32 devices in a mesh: dp: 8 (over y, x, core), fsdp: 4 (over z).
Axes of the slice: x: 2, y: 2, z: 4, core: 2. Of those that a mesh axis runs over, the one named last changes fastest.
Arguments:
- queries: bfloat16 [8192, 2048], P(('dp', 'fsdp')), may hold values from -600 to 600
- w_kv: bfloat16 [2, 2048, 896], P(None, 'fsdp'), may hold values from -0.1875 to 0.1875
- encodings: bfloat16 [12288, 896], P(('dp', 'fsdp')), may hold values from -6 to 6
- counts: int32 [32], P(('dp', 'fsdp')), may hold values from 48 to 384, as said below
- owner_rank: int32 [12288], P(('dp', 'fsdp')), may hold values from 0 to 7, as said below
- owner_span: int32 [12288], P(('dp', 'fsdp')), may hold values from 0 to 3, as said below
- grad_ctx: bfloat16 [8192, 2048], P(('dp', 'fsdp')), may hold values from -6 to 6
Outputs:
- grad_queries: bfloat16 [8192, 2048], P(('dp', 'fsdp'))
- grad_value: bfloat16 [2048, 896], P('fsdp')
The draws below stay inside these ranges and needn't reach their ends.
Inputs may be any that keep to these rules, and one draw needn't show every extreme that they name: `counts`: each count is 384 divided by 1, 2, 4 or 8; among the devices of equal fsdp index one holds 384. `owner_rank`: among the live rows of one device at most 48 name the same owner; a device whose count is 384 names every owner exactly 48 times. `owner_span`: every span of every decoder device is named by at least one live row of a device with equal fsdp index.
All inputs are finite; a program needn't handle non-finite values.
Results may differ from the reference program's by a relative error of at most 0.023.
Values may be sent and summed in bfloat16 or wider, within the bound.
A program may use at most 64 MiB of HBM per device.

```python
import jax
import jax.numpy as jnp
from jax import lax

HEADS = 16
HEAD_DIM = 128
ENC = 896
SPAN = 64
TOK_DEV = 256
ENC_ROWS_DEV = 384
HW = 2048
SPANS_DEV = 4
PAIR_CAP = 48
TOKENS = 8192
ENC_ROWS = 12288
N_DP = 8
N_FSDP = 4
DEVICES = 32


def routing_tables(key):
    base = jax.random.fold_in(key, 11)
    key_shift, key_full, key_order, key_offset = jax.random.split(base, 4)
    shifts = jax.random.randint(key_shift, (N_DP, N_FSDP), 0, 4)
    full_index = jax.random.randint(key_full, (N_FSDP,), 0, N_DP)
    shifts = jnp.where(jnp.arange(N_DP)[:, None] == full_index[None, :], 0, shifts)
    live_counts = jnp.right_shift(jnp.full((N_DP, N_FSDP), ENC_ROWS_DEV, jnp.int32), shifts.astype(jnp.int32))
    order_scores = jax.random.randint(key_order, (DEVICES, ENC_ROWS_DEV), 0, 4096) * ENC_ROWS_DEV + jnp.arange(ENC_ROWS_DEV)[None, :]
    ordering = jnp.argsort(order_scores, axis=1, stable=True).astype(jnp.int32)
    offsets = jax.random.randint(key_offset, (DEVICES, 1), 0, SPANS_DEV)
    ranks = (ordering // PAIR_CAP).reshape(-1).astype(jnp.int32)
    spans = ((ordering + offsets) % SPANS_DEV).reshape(-1).astype(jnp.int32)
    return (live_counts.reshape(-1).astype(jnp.int32), ranks, spans)


def draw_counts(key, part):
    return routing_tables(key)[0]


def draw_owner_rank(key, part):
    return routing_tables(key)[1]


def draw_owner_span(key, part):
    return routing_tables(key)[2]


def draw_queries(key, part):
    base = jax.random.fold_in(key, 3)
    key_main = jax.random.fold_in(base, 0)
    values = jnp.clip(jax.random.normal(key_main, (TOKENS, HW), jnp.float32), -6.0, 6.0)
    return values.astype(jnp.bfloat16)


def raised(values, stream_key, source, target, parts, factor):
    owner, partner = [(jnp.arange(values.shape[dim]) // (values.shape[dim] // parts)).reshape([-1 if axis == dim else 1 for axis in range(values.ndim)]) for dim in (source, target)]
    chosen = jax.random.permutation(stream_key, parts)[partner]
    strong = (owner == chosen) | (owner == (partner + parts // 2) % parts)
    return jnp.where(strong, factor * values, values)


def steps_of(key, extent, cuts, least, top_value):
    gain, own = 1.0, jax.random.fold_in(key, 6)
    for position, parts in cuts:
        draws = jnp.exp(jax.random.uniform(jax.random.fold_in(own, position), (parts,), jnp.float32, least / len(cuts), top_value / len(cuts)))
        gain = gain * jnp.repeat(draws, extent[position] // parts).reshape([-1 if axis == position else 1 for axis in range(len(extent))])
    return gain


def gaussian(stream_key, shape, deviation, limit, pieces=(), kind=jnp.bfloat16):
    drawn = jax.random.normal(stream_key, shape, jnp.float32) * deviation
    if len(pieces) > 0:
        drawn = steps_of(stream_key, shape, pieces, -0.22, 0.18) * drawn
    return jnp.clip(drawn, min=-limit, max=limit).astype(kind)


def heavy_noise(rng, shape, deviation, reach, cuts, heavy, kind=jnp.bfloat16):
    array = deviation * jax.random.normal(rng, shape, jnp.float32)
    if cuts:
        array = array * steps_of(rng, shape, cuts, -0.22, 0.18)
    return jnp.clip(raised(array, jax.random.fold_in(rng, 3), *heavy), -reach, reach).astype(kind)


def setup_inputs(seed: int = 0) -> dict:
    key_list = jax.random.split(jax.random.key(seed), 8)
    queries = draw_queries(jax.random.fold_in(key_list[7], 71), 0)
    w_kv = gaussian(key_list[1], (2, HW, ENC), ENC ** -0.5, 0.1875, ((1, 4),))
    encodings = gaussian(key_list[2], (ENC_ROWS, ENC), 1.0, 6.0, ((0, 32),))
    counts = draw_counts(jax.random.fold_in(key_list[7], 71), 0)
    owner_rank = draw_owner_rank(jax.random.fold_in(key_list[7], 71), 0)
    owner_span = draw_owner_span(jax.random.fold_in(key_list[7], 71), 0)
    grad_ctx = heavy_noise(key_list[6], (TOKENS, HW), 1.0, 6.0, ((0, 32),), (0, 1, 32, 2.75))
    return dict(queries=queries, w_kv=w_kv, encodings=encodings, counts=counts, owner_rank=owner_rank, owner_span=owner_span, grad_ctx=grad_ctx)


def pack_rows(enc_rows, live_count, rank_rows, span_rows):
    row_total = enc_rows.shape[0]
    pair_slots = row_total // N_DP
    live_rows = jnp.arange(row_total, dtype=jnp.int32) < live_count
    hit_table = ((rank_rows[:, None] == jnp.arange(N_DP, dtype=jnp.int32)[None, :]) & live_rows[:, None]).astype(jnp.int32)
    before_hits = jnp.cumsum(hit_table, axis=0) - hit_table
    slot_index = jnp.sum(before_hits * hit_table, axis=1)
    target = jnp.where(live_rows, rank_rows * pair_slots + slot_index, N_DP * pair_slots).astype(jnp.int32)
    buffer = jnp.zeros((N_DP * pair_slots, enc_rows.shape[1]), enc_rows.dtype).at[target].set(enc_rows, mode="drop")
    tag_buffer = jnp.full((N_DP * pair_slots,), -1, jnp.int32).at[target].set(span_rows, mode="drop")
    return buffer.reshape(N_DP, pair_slots, enc_rows.shape[1]), tag_buffer.reshape(N_DP, pair_slots)


def device_step(total, inputs, w_kv):
    query_rows, cotangent, received, tag_rows = inputs
    contract = (((1,), (1,)), ((), ()))
    keys = lax.dot_general(received, w_kv[0], contract, preferred_element_type=jnp.float32).astype(jnp.bfloat16)
    values = lax.dot_general(received, w_kv[1], contract, preferred_element_type=jnp.float32).astype(jnp.bfloat16)
    token_total = query_rows.shape[0]
    slot_total = received.shape[0]
    scale = 1.0 / (HEAD_DIM ** 0.5)
    query_heads = query_rows.reshape(token_total, HEADS, HEAD_DIM).astype(jnp.float32)
    key_heads = keys.reshape(slot_total, HEADS, HEAD_DIM).astype(jnp.float32)
    value_heads = values.reshape(slot_total, HEADS, HEAD_DIM).astype(jnp.float32)
    grad_heads = cotangent.reshape(token_total, HEADS, HEAD_DIM).astype(jnp.float32)
    scores = jnp.einsum("thd,khd->htk", query_heads, key_heads) * scale
    token_span = jnp.arange(token_total, dtype=jnp.int32) // SPAN
    allowed = (token_span[:, None] == tag_rows[None, :])[None]
    masked = jnp.where(allowed, scores, -1e30)
    highest = jnp.max(masked, axis=-1, keepdims=True)
    weights = jnp.where(allowed, jnp.exp(masked - highest), 0.0)
    probs = weights / jnp.sum(weights, axis=-1, keepdims=True)
    probs_low = probs.astype(jnp.bfloat16)
    context = jnp.einsum("htk,khd->thd", probs_low.astype(jnp.float32), value_heads)
    dprob = jnp.einsum("thd,khd->htk", grad_heads, value_heads)
    delta = jnp.transpose(jnp.sum(grad_heads * context, axis=-1))[:, :, None]
    dscore = (probs * (dprob - delta)).astype(jnp.bfloat16)
    grad_query = (jnp.einsum("htk,khd->thd", dscore.astype(jnp.float32), key_heads) * scale).astype(jnp.bfloat16)
    dval = jnp.einsum("htk,thd->khd", probs_low.astype(jnp.float32), grad_heads).astype(jnp.bfloat16)
    dval = dval.reshape(slot_total, HW)
    partial_value = lax.dot_general(dval, received, (((0,), (0,)), ((), ())), preferred_element_type=jnp.float32)
    total = total + partial_value.astype(jnp.bfloat16).astype(jnp.float32)
    return total, grad_query.reshape(token_total, HW)


def reference(queries, w_kv, encodings, counts, owner_rank, owner_span, grad_ctx):
    device_total = N_DP * N_FSDP
    enc_blocks = encodings.reshape(N_DP, N_FSDP, ENC_ROWS_DEV, ENC)
    count_blocks = counts.reshape(N_DP, N_FSDP)
    rank_blocks = owner_rank.reshape(N_DP, N_FSDP, ENC_ROWS_DEV)
    span_blocks = owner_span.reshape(N_DP, N_FSDP, ENC_ROWS_DEV)
    packer = jax.vmap(jax.vmap(pack_rows))
    sent, sent_tags = packer(enc_blocks, count_blocks, rank_blocks, span_blocks)
    received = jnp.transpose(sent, (2, 1, 0, 3, 4)).reshape(device_total, ENC_ROWS_DEV, ENC)
    tags = jnp.transpose(sent_tags, (2, 1, 0, 3)).reshape(device_total, ENC_ROWS_DEV)
    query_blocks = queries.reshape(device_total, TOK_DEV, HW)
    grad_blocks = grad_ctx.reshape(device_total, TOK_DEV, HW)
    start_total = jnp.zeros((HW, ENC), jnp.float32)
    final_total, grad_queries = lax.scan(partial_fn(w_kv), start_total, (query_blocks, grad_blocks, received, tags))
    grad_value = (final_total / N_DP).astype(jnp.bfloat16)
    return grad_queries.reshape(TOKENS, HW), grad_value


def partial_fn(w_kv):
    def stepper(total, inputs):
        return device_step(total, inputs, w_kv)
    return stepper
```

```python
import jax
import jax.numpy as jnp
from jax import lax
from jax.sharding import PartitionSpec as P

HEADS = 16
HEAD_DIM = 128
SPAN = 64


def pack_rows(enc_rows, live_count, rank_rows, span_rows, dp_count):
    row_total = enc_rows.shape[0]
    pair_slots = row_total // dp_count
    rows = jnp.arange(row_total, dtype=jnp.int32)
    live_rows = rows < live_count
    hits = (rank_rows[:, None] == jnp.arange(dp_count, dtype=jnp.int32)[None, :]) & live_rows[:, None]
    earlier = (rows[None, :] < rows[:, None]).astype(jnp.bfloat16)
    before = jnp.dot(earlier, hits.astype(jnp.bfloat16), preferred_element_type=jnp.float32)
    slot_index = jnp.sum(jnp.where(hits, before, 0.0), axis=1).astype(jnp.int32)
    target = jnp.where(live_rows, rank_rows * pair_slots + slot_index, -1)
    placed = target[None, :] == rows[:, None]
    buffer = jnp.dot(
        placed.astype(jnp.bfloat16), enc_rows, preferred_element_type=jnp.float32
    ).astype(jnp.bfloat16)
    tag_buffer = jnp.sum(jnp.where(placed, span_rows[None, :] + 1, 0), axis=1) - 1
    return (
        buffer.reshape(dp_count, pair_slots, enc_rows.shape[1]),
        tag_buffer.reshape(dp_count, pair_slots),
    )


def local(queries, w_kv, encodings, counts, owner_rank, owner_span, grad_ctx):
    dp_count = lax.axis_size("dp")
    slot_total = encodings.shape[0]
    width = encodings.shape[1]
    buffer, tag_buffer = pack_rows(encodings, counts[0], owner_rank, owner_span, dp_count)
    arrived, arrived_tags = (
        lax.all_to_all(buffer, "dp", split_axis=0, concat_axis=0, tiled=True),
        lax.all_to_all(tag_buffer, "dp", split_axis=0, concat_axis=0, tiled=True),
    )
    received = arrived.reshape(slot_total, width)
    tag_rows = arrived_tags.reshape(slot_total)
    contract = (((1,), (1,)), ((), ()))

    def project_one(piece):
        return lax.dot_general(
            received, piece, contract, preferred_element_type=jnp.float32
        ).astype(jnp.bfloat16)

    keys = project_one(lax.all_gather(w_kv[0], "fsdp", axis=0, tiled=True))
    values = project_one(lax.all_gather(w_kv[1], "fsdp", axis=0, tiled=True))
    token_total = queries.shape[0]
    scale = 1.0 / HEAD_DIM**0.5
    query_heads = queries.reshape(token_total, HEADS, HEAD_DIM)
    key_heads = keys.reshape(slot_total, HEADS, HEAD_DIM)
    value_heads = values.reshape(slot_total, HEADS, HEAD_DIM)
    grad_heads = grad_ctx.reshape(token_total, HEADS, HEAD_DIM)
    scores = (
        jnp.einsum("thd,khd->htk", query_heads, key_heads, preferred_element_type=jnp.float32)
        * scale
    )
    token_span = jnp.arange(token_total, dtype=jnp.int32) // SPAN
    allowed = (token_span[:, None] == tag_rows[None, :])[None]
    masked = jnp.where(allowed, scores, -1e30)
    highest = jnp.max(masked, axis=-1, keepdims=True)
    weights = jnp.where(allowed, jnp.exp(masked - highest), 0.0)
    probs = weights / jnp.sum(weights, axis=-1, keepdims=True)
    probs_low = probs.astype(jnp.bfloat16)
    context = jnp.einsum("htk,khd->thd", probs_low, value_heads, preferred_element_type=jnp.float32)
    dprob = jnp.einsum("thd,khd->htk", grad_heads, value_heads, preferred_element_type=jnp.float32)
    delta = jnp.transpose(jnp.sum(grad_heads.astype(jnp.float32) * context, axis=-1))[:, :, None]
    dscore = (probs * (dprob - delta)).astype(jnp.bfloat16)
    grad_query = (
        jnp.einsum("htk,khd->thd", dscore, key_heads, preferred_element_type=jnp.float32) * scale
    )
    grad_queries = grad_query.astype(jnp.bfloat16).reshape(token_total, HEADS * HEAD_DIM)
    dval = jnp.einsum("htk,thd->khd", probs_low, grad_heads, preferred_element_type=jnp.float32)
    dval = dval.astype(jnp.bfloat16).reshape(slot_total, HEADS * HEAD_DIM)
    piece = dval
    shard_sum = lax.psum_scatter(
        lax.dot_general(
            piece, received, (((0,), (0,)), ((), ())), preferred_element_type=jnp.float32
        ).astype(jnp.bfloat16),
        "fsdp",
        scatter_dimension=0,
        tiled=True,
    )
    group_sum = lax.psum(shard_sum, "dp").astype(jnp.float32)
    grad_value = (group_sum / dp_count).astype(jnp.bfloat16)
    return (grad_queries, grad_value)


def solution(mesh):
    in_specs = (
        P(("dp", "fsdp"), None),
        P(None, "fsdp", None),
        P(("dp", "fsdp"), None),
        P(("dp", "fsdp")),
        P(("dp", "fsdp")),
        P(("dp", "fsdp")),
        P(("dp", "fsdp"), None),
    )
    out_specs = (P(("dp", "fsdp"), None), P("fsdp", None))
    return jax.shard_map(local, mesh=mesh, in_specs=in_specs, out_specs=out_specs, check_vma=False)
```
